32 devices in a mesh: gx: 2 (over x), gy: 2 (over y), gz: 8 (over z, core).
Axes of the slice: x: 2, y: 2, z: 4, core: 2. Of those that a mesh axis runs over, the one named last changes fastest.
Arguments:
- seeds: float32 [2, 2, 8, 64, 256], P('gx', 'gy', 'gz'), may hold values from -6 to 6
- schur: float32 [2, 2, 8, 1152, 1152], P('gx', 'gy', 'gz')
- inverse: float32 [2, 2, 8, 1152, 1152], P('gx', 'gy', 'gz')
- deluxe: float32 [2, 2, 8, 1152], P('gx', 'gy', 'gz'), may hold values from 0.5 to 2
- orders: int32 [2, 2, 8], P('gx', 'gy', 'gz'), may hold values from 360 to 1152, as said below
- links: int32 [2, 2, 8, 1152], P('gx', 'gy', 'gz'), may hold values from 0 to 1791, as said below
Outputs:
- adjoint: float32 [2, 2, 8, 64, 256], P('gx', 'gy', 'gz')
- residual: float32 [2, 2, 8, 64, 256], P('gx', 'gy', 'gz')
The draws below stay inside these ranges and needn't reach their ends.
Inputs may be any that keep to these rules, and one draw needn't show every extreme that they name: `orders`: each value lies in 360 to 1152; some subdomain has exactly 1152. `links`: A slot names only a subdomain that exists in the grid; entries at rows at or beyond the subdomain's order are arbitrary.
All inputs are finite; a program needn't handle non-finite values.
Results may differ from the reference program's by a relative error of at most 0.00015.
Values sent between devices are 32-bit elements; how exact they have to be, the bound alone decides.
A program may use at most 64 MiB of HBM per device.

```python
import math
import jax
import jax.numpy as jnp
from jax import lax

P_SIZE = 1152
R = 64
OWN = 256
GX = 2
GY = 2
GZ = 8


def diagonal_part(key):
    return jax.random.uniform(jax.random.fold_in(key, 11), (GX, GY, GZ, P_SIZE), jnp.float32, 2.0, 4.0)


def draw_schur(key, part):
    diag_values = diagonal_part(key)
    spread = jax.random.normal(jax.random.fold_in(key, 12), (GX, GY, GZ, P_SIZE, P_SIZE), jnp.float32) * (0.8 / math.sqrt(P_SIZE))
    return spread + jnp.eye(P_SIZE, dtype=jnp.float32) * diag_values[..., None, :]


def draw_inverse(key, part):
    diag_values = diagonal_part(key)
    spread = jax.random.normal(jax.random.fold_in(key, 13), (GX, GY, GZ, P_SIZE, P_SIZE), jnp.float32) * (0.12 / math.sqrt(P_SIZE))
    return spread + jnp.eye(P_SIZE, dtype=jnp.float32) * (1.0 / diag_values)[..., None, :]


def draw_orders(key, part):
    count = GX * GY * GZ
    lowest = P_SIZE * 5 // 16
    values = jax.random.randint(jax.random.fold_in(key, 21), (count,), lowest, P_SIZE + 1)
    first = jax.random.randint(jax.random.fold_in(key, 22), (), 0, count)
    second = (first + 1 + jax.random.randint(jax.random.fold_in(key, 23), (), 0, count - 1)) % count
    values = values.at[first].set(P_SIZE).at[second].set(lowest)
    return values.reshape(GX, GY, GZ).astype(jnp.int32)


def draw_links(key, part):
    shape = (GX, GY, GZ, P_SIZE)
    slot = jax.random.randint(jax.random.fold_in(key, 31), shape, 0, 7)
    row = jax.random.randint(jax.random.fold_in(key, 32), shape, 0, OWN)
    first = lax.broadcasted_iota(jnp.int32, shape, 0)
    second = lax.broadcasted_iota(jnp.int32, shape, 1)
    third = lax.broadcasted_iota(jnp.int32, shape, 2)
    valid = jnp.where(slot == 1, first > 0, True)
    valid = valid & jnp.where(slot == 2, first < GX - 1, True)
    valid = valid & jnp.where(slot == 3, second > 0, True)
    valid = valid & jnp.where(slot == 4, second < GY - 1, True)
    valid = valid & jnp.where(slot == 5, third > 0, True)
    valid = valid & jnp.where(slot == 6, third < GZ - 1, True)
    slot = jnp.where(valid, slot, 0)
    values = slot * OWN + row
    values = values.at[0, 0, 0, 0].set(7 * OWN - 1).at[0, 0, 0, 1].set(0)
    return values.astype(jnp.int32)


def steps_of(key, shape, split, smallest, largest):
    gain = 1.0
    for axis_at, shards_of in split:
        steps = jax.random.uniform(jax.random.fold_in(jax.random.fold_in(key, 6), axis_at), (shards_of,), jnp.float32, smallest / len(split), largest / len(split))
        gain = gain * jnp.repeat(jnp.exp(steps), shape[axis_at] // shards_of).reshape((-1,) + (1,) * (len(shape) - 1 - axis_at))
    return gain


def normal_values(key, shape, width, limit, shards=(), kind=jnp.bfloat16):
    loudness = steps_of(key, shape, shards, -0.22, 0.18) if shards else 1.0
    result = jax.random.normal(key, shape, jnp.float32) * width * loudness
    return jnp.minimum(jnp.maximum(result, -limit), limit).astype(kind)


def setup_inputs(seed: int = 0) -> dict:
    splits = jax.random.split(jax.random.key(seed), 7)
    return {
        "seeds": normal_values(splits[0], (GX, GY, GZ, R, OWN), 1.0, 6.0, ((0, 2), (1, 2), (2, 8)), jnp.float32),
        "schur": draw_schur(jax.random.fold_in(splits[6], 71), 0),
        "inverse": draw_inverse(jax.random.fold_in(splits[6], 71), 0),
        "deluxe": jnp.clip(jnp.exp(math.log(2.0) - 1.3862944 * jax.random.uniform(splits[3], (GX, GY, GZ, P_SIZE), jnp.float32) ** steps_of(splits[3], (GX, GY, GZ, P_SIZE), ((0, 2), (1, 2), (2, 8)), -0.2, 0.2)), 0.5, 2.0),
        "orders": draw_orders(jax.random.fold_in(splits[6], 71), 0),
        "links": draw_links(jax.random.fold_in(splits[6], 71), 0),
    }


def owner_rows(links):
    shape = (GX, GY, GZ, P_SIZE)
    first = lax.broadcasted_iota(jnp.int32, shape, 0)
    second = lax.broadcasted_iota(jnp.int32, shape, 1)
    third = lax.broadcasted_iota(jnp.int32, shape, 2)
    slot = links // OWN
    row = links % OWN
    first = first + jnp.where(slot == 2, 1, 0) - jnp.where(slot == 1, 1, 0)
    second = second + jnp.where(slot == 4, 1, 0) - jnp.where(slot == 3, 1, 0)
    third = third + jnp.where(slot == 6, 1, 0) - jnp.where(slot == 5, 1, 0)
    flat = (first * GY + second) * GZ + third
    return (flat * OWN + row).astype(jnp.int32).reshape(GX * GY * GZ, P_SIZE)


def apply(vector, matrices, weight, rows):
    local = jnp.transpose(vector[:, rows], (1, 0, 2)) * weight[:, None, :]
    image = jnp.einsum("drp,dpq->drq", local, matrices, precision=lax.Precision.HIGHEST) * weight[:, None, :]
    image = jnp.transpose(image, (1, 0, 2)).reshape(R, -1)
    return jnp.zeros_like(vector).at[:, rows.reshape(-1)].add(image)


def reference(seeds, schur, inverse, deluxe, orders, links):
    count = GX * GY * GZ
    rows = owner_rows(links)
    mask = (jnp.arange(P_SIZE, dtype=jnp.int32)[None, :] < orders.reshape(count, 1)).astype(jnp.float32)
    weight = mask * deluxe.reshape(count, P_SIZE)
    schur_flat = schur.reshape(count, P_SIZE, P_SIZE)
    inverse_flat = inverse.reshape(count, P_SIZE, P_SIZE)
    gradient = jnp.transpose(seeds, (3, 0, 1, 2, 4)).reshape(R, count * OWN)
    adjoint1 = apply(gradient, inverse_flat, weight, rows)
    residual = gradient - apply(adjoint1, schur_flat, mask, rows)
    adjoint = adjoint1 + apply(residual, inverse_flat, weight, rows)

    def back(vector):
        return jnp.transpose(vector.reshape(R, GX, GY, GZ, OWN), (1, 2, 3, 0, 4))

    return back(adjoint), back(residual)
```

```python
import functools

import jax
import jax.numpy as jnp
from jax import lax
from jax.experimental import pallas as pl
from jax.experimental.pallas import tpu as pltpu
from jax.sharding import PartitionSpec as P

MESH = pl.DeviceIdType.MESH
F32 = jnp.float32
BF16 = jnp.bfloat16
AXES = ("gx", "gy", "gz")


def slot_plan(sizes):
    remote, kept = [], [0]
    for at, size in enumerate(sizes):
        here = 1 + len(remote)
        if size == 2:
            remote.append((at, 0, here))
            kept += [here, here]
        else:
            remote += [(at, -1, here + 1), (at, 1, here)]
            kept += [here, here + 1]
    return remote, kept


def split(value):
    high = value.astype(BF16)
    return high, (value - high.astype(F32)).astype(BF16)


def kernel(
    sizes,
    remote,
    kept,
    seeds,
    schur_hbm,
    inverse_hbm,
    deluxe_ref,
    order_ref,
    links_ref,
    adjoint_ref,
    residual_ref,
    schur,
    inverse,
    schur_high,
    schur_low,
    inverse_high,
    inverse_low,
    pick,
    landed,
    contrib,
    first,
    stacked,
    local,
    load_sem,
    send_sem,
    recv_sem,
):
    rows, owned = seeds.shape
    order_count = schur.shape[0]
    at = [lax.axis_index(name) for name in AXES]

    def neighbour(slot):
        axis, step, _ = remote[slot - 1]
        there = list(at)
        there[axis] = 1 - at[axis] if step == 0 else at[axis] + step
        return tuple(there)

    def present(slot, run, otherwise=None):
        axis, step, _ = remote[slot - 1]
        if step == 0:
            run()
            return
        there = at[axis] > 0 if step < 0 else at[axis] < sizes[axis] - 1
        pl.when(there)(run)
        if otherwise is not None:
            pl.when(jnp.logical_not(there))(otherwise)

    slots = range(1, len(remote) + 1)

    def copy_to(stage, slot, source):
        there = remote[slot - 1][2]
        return pltpu.make_async_remote_copy(
            src_ref=source,
            dst_ref=landed.at[stage, there - 1],
            send_sem=send_sem.at[stage, slot - 1],
            recv_sem=recv_sem.at[stage, there - 1],
            device_id=neighbour(slot),
            device_id_type=MESH,
        )

    def copy_from(stage, slot):
        return pltpu.make_async_remote_copy(
            src_ref=landed.at[stage, slot - 1],
            dst_ref=landed.at[stage, slot - 1],
            send_sem=send_sem.at[stage, slot - 1],
            recv_sem=recv_sem.at[stage, slot - 1],
            device_id=neighbour(slot),
            device_id_type=MESH,
        )

    load_inverse = pltpu.make_async_copy(inverse_hbm, inverse, load_sem.at[0])
    load_schur = pltpu.make_async_copy(schur_hbm, schur, load_sem.at[1])
    load_inverse.start()
    load_schur.start()

    barrier = pltpu.get_barrier_semaphore()
    for slot in slots:
        present(
            slot,
            lambda slot=slot: pl.semaphore_signal(
                barrier, inc=1, device_id=neighbour(slot), device_id_type=MESH
            ),
        )
    peers = 0
    for axis, step, _ in remote:
        if step == 0:
            peers += 1
        else:
            there = at[axis] > 0 if step < 0 else at[axis] < sizes[axis] - 1
            peers += jnp.where(there, 1, 0)
    pl.semaphore_wait(barrier, peers)

    def send_all(stage, source):
        for slot in slots:
            present(slot, lambda slot=slot: copy_to(stage, slot, source).start())

    send_all(0, seeds)

    for slot in slots:

        def clear(slot=slot):
            for stage in range(6):
                landed[stage, slot - 1] = jnp.zeros((rows, owned), F32)

        present(slot, lambda: None, clear)

    links = links_ref[0, 0]
    place = links
    for slot, here in enumerate(kept):
        if here != slot:
            inside = jnp.logical_and(links >= slot * owned, links < (slot + 1) * owned)
            place = jnp.where(inside, links + (here - slot) * owned, place)
    column = lax.broadcasted_iota(jnp.int32, (1, order_count), 1)
    place = jnp.where(column < order_ref[0, 0, 0], place, -1)
    index = lax.broadcasted_iota(jnp.int32, (owned, 1), 0)
    for slot in range(len(remote) + 1):
        pick[slot] = jnp.where(place == index + slot * owned, 1.0, 0.0).astype(BF16)
    weight = deluxe_ref[0, 0]

    def prepare(matrix, high, low):
        step = 128

        def some(i, carry):
            part = pl.ds(pl.multiple_of(i * step, step), step)
            high[part, :], low[part, :] = split(matrix[part, :])
            return carry

        lax.fori_loop(0, order_count // step, some, 0)

    def gather(stage, own):
        def add(slot, block):
            high, low = split(block)
            both = jnp.concatenate([high, low], axis=0)
            part = jnp.dot(both, pick[slot], preferred_element_type=F32)
            if slot == 0:
                local[...] = part
            else:
                local[...] += part

        add(0, own)
        for slot in reversed(slots):
            present(slot, lambda slot=slot: copy_from(stage, slot).wait_recv())
            add(slot, landed[stage, slot - 1])

    def apply(turn, own, high, low, scaled):
        gather(2 * turn, own)
        value = local[:rows] + local[rows:]
        if scaled:
            value = value * weight
        value_high, value_low = split(value)
        stacked[:rows] = value_high
        stacked[rows:] = value_low
        main = jnp.dot(stacked[...], high[...], preferred_element_type=F32)
        rest = jnp.dot(stacked[:rows], low[...], preferred_element_type=F32)
        image = main[:rows] + main[rows:] + rest
        if scaled:
            image = image * weight
        image_high, image_low = split(image)
        stacked[:rows] = image_high
        stacked[rows:] = image_low

        def scatter(slot):
            both = lax.dot_general(
                stacked[...], pick[slot], (((1,), (1,)), ((), ())), preferred_element_type=F32
            )
            return both[:rows] + both[rows:]

        for slot in slots:
            contrib[turn, slot - 1] = scatter(slot)
            present(
                slot,
                lambda slot=slot: copy_to(2 * turn + 1, slot, contrib.at[turn, slot - 1]).start(),
            )
        return scatter(0)

    def returned(turn, total):
        for slot in reversed(slots):
            present(slot, lambda slot=slot: copy_from(2 * turn + 1, slot).wait_recv())
            total = total + landed[2 * turn + 1, slot - 1]
        return total

    load_inverse.wait()
    prepare(inverse, inverse_high, inverse_low)
    own = apply(0, seeds[...], inverse_high, inverse_low, True)
    load_schur.wait()
    prepare(schur, schur_high, schur_low)
    first[...] = returned(0, own)
    send_all(2, first)

    own = apply(1, first[...], schur_high, schur_low, False)
    residual_ref[...] = seeds[...] - returned(1, own)
    send_all(4, residual_ref)

    own = apply(2, residual_ref[...], inverse_high, inverse_low, True)
    adjoint_ref[...] = first[...] + returned(2, own)

    for stage, source in enumerate((seeds, None, first, None, residual_ref, None)):
        for slot in slots:
            block = contrib.at[stage // 2, slot - 1] if source is None else source
            present(
                slot,
                lambda stage=stage, slot=slot, block=block: copy_to(stage, slot, block).wait_send(),
            )


def solution(mesh):
    sizes = tuple(mesh.shape[name] for name in AXES)
    remote, kept = slot_plan(sizes)

    def body(seeds, schur, inverse, deluxe, orders, links):
        rows, owned = seeds.shape[3:]
        order_count = schur.shape[3]
        count = len(remote)
        vmem = pl.BlockSpec(memory_space=pltpu.VMEM)
        hbm = pl.BlockSpec(memory_space=pl.ANY)
        result = jax.ShapeDtypeStruct((rows, owned), F32)
        square = (order_count, order_count)
        adjoint, residual = pl.pallas_call(
            functools.partial(kernel, sizes, remote, kept),
            out_shape=(result, result),
            in_specs=[vmem, hbm, hbm, vmem, pl.BlockSpec(memory_space=pltpu.SMEM), vmem],
            out_specs=(vmem, vmem),
            scratch_shapes=[
                pltpu.VMEM(square, F32),
                pltpu.VMEM(square, F32),
                pltpu.VMEM(square, BF16),
                pltpu.VMEM(square, BF16),
                pltpu.VMEM(square, BF16),
                pltpu.VMEM(square, BF16),
                pltpu.VMEM((count + 1, owned, order_count), BF16),
                pltpu.VMEM((6, count, rows, owned), F32),
                pltpu.VMEM((3, count, rows, owned), F32),
                pltpu.VMEM((rows, owned), F32),
                pltpu.VMEM((2 * rows, order_count), BF16),
                pltpu.VMEM((2 * rows, order_count), F32),
                pltpu.SemaphoreType.DMA((2,)),
                pltpu.SemaphoreType.DMA((6, count)),
                pltpu.SemaphoreType.DMA((6, count)),
            ],
            compiler_params=pltpu.CompilerParams(
                collective_id=0, has_side_effects=True, vmem_limit_bytes=60 * 1024 * 1024
            ),
        )(
            seeds[0, 0, 0],
            schur[0, 0, 0],
            inverse[0, 0, 0],
            deluxe[0],
            orders,
            links[0],
        )
        return adjoint[None, None, None], residual[None, None, None]

    in_specs = (
        P("gx", "gy", "gz", None, None),
        P("gx", "gy", "gz", None, None),
        P("gx", "gy", "gz", None, None),
        P("gx", "gy", "gz", None),
        P("gx", "gy", "gz"),
        P("gx", "gy", "gz", None),
    )
    out_specs = (P("gx", "gy", "gz", None, None), P("gx", "gy", "gz", None, None))
    return jax.shard_map(body, mesh=mesh, in_specs=in_specs, out_specs=out_specs, check_vma=False)
```

```python
import functools

import jax
import jax.numpy as jnp
from jax import lax
from jax.experimental import pallas as pl
from jax.experimental.pallas import tpu as pltpu
from jax.sharding import PartitionSpec as P

MESH = pl.DeviceIdType.MESH
F32 = jnp.float32
BF16 = jnp.bfloat16
AXES = ("gx", "gy", "gz")


def slot_plan(sizes):
    remote, kept = [], [0]
    for at, size in enumerate(sizes):
        here = 1 + len(remote)
        if size == 2:
            remote.append((at, 0, here))
            kept += [here, here]
        else:
            remote += [(at, -1, here + 1), (at, 1, here)]
            kept += [here, here + 1]
    return remote, kept


def split(value):
    high = value.astype(BF16)
    return high, (value - high.astype(F32)).astype(BF16)


def kernel(
    sizes,
    remote,
    kept,
    seeds,
    schur_hbm,
    inverse_hbm,
    deluxe_ref,
    order_ref,
    links_ref,
    adjoint_ref,
    residual_ref,
    schur,
    inverse,
    schur_high,
    schur_low,
    inverse_high,
    inverse_low,
    pick,
    place_back,
    landed,
    contrib,
    first,
    stacked,
    images,
    local,
    load_sem,
    send_sem,
    recv_sem,
):
    rows, owned = seeds.shape
    order_count = schur.shape[0]
    wide = 384 if order_count % 384 == 0 else 128
    at = [lax.axis_index(name) for name in AXES]

    def neighbour(slot):
        axis, step, _ = remote[slot - 1]
        there = list(at)
        there[axis] = 1 - at[axis] if step == 0 else at[axis] + step
        return tuple(there)

    def present(slot, run, otherwise=None):
        axis, step, _ = remote[slot - 1]
        if step == 0:
            run()
            return
        there = at[axis] > 0 if step < 0 else at[axis] < sizes[axis] - 1
        pl.when(there)(run)
        if otherwise is not None:
            pl.when(jnp.logical_not(there))(otherwise)

    slots = range(1, len(remote) + 1)

    def copy_to(stage, slot, source):
        there = remote[slot - 1][2]
        return pltpu.make_async_remote_copy(
            src_ref=source,
            dst_ref=landed.at[stage, there - 1],
            send_sem=send_sem.at[stage, slot - 1],
            recv_sem=recv_sem.at[stage, there - 1],
            device_id=neighbour(slot),
            device_id_type=MESH,
        )

    def copy_from(stage, slot):
        return pltpu.make_async_remote_copy(
            src_ref=landed.at[stage, slot - 1],
            dst_ref=landed.at[stage, slot - 1],
            send_sem=send_sem.at[stage, slot - 1],
            recv_sem=recv_sem.at[stage, slot - 1],
            device_id=neighbour(slot),
            device_id_type=MESH,
        )

    load_inverse = pltpu.make_async_copy(inverse_hbm, inverse, load_sem.at[0])
    load_schur = pltpu.make_async_copy(schur_hbm, schur, load_sem.at[1])
    load_inverse.start()

    barrier = pltpu.get_barrier_semaphore()
    for slot in slots:
        present(
            slot,
            lambda slot=slot: pl.semaphore_signal(
                barrier, inc=1, device_id=neighbour(slot), device_id_type=MESH
            ),
        )
    peers = 0
    for axis, step, _ in remote:
        if step == 0:
            peers += 1
        else:
            there = at[axis] > 0 if step < 0 else at[axis] < sizes[axis] - 1
            peers += jnp.where(there, 1, 0)
    pl.semaphore_wait(barrier, peers)

    def send_all(stage, source):
        for slot in slots:
            present(slot, lambda slot=slot: copy_to(stage, slot, source).start())

    send_all(0, seeds)

    for slot in slots:

        def clear(slot=slot):
            for stage in range(6):
                landed[stage, slot - 1] = jnp.zeros((rows, owned), F32)

        present(slot, lambda: None, clear)

    links = links_ref[0]
    place = links
    for slot, here in enumerate(kept):
        if here != slot:
            inside = jnp.logical_and(links >= slot * owned, links < (slot + 1) * owned)
            place = jnp.where(inside, links + (here - slot) * owned, place)
    column = lax.broadcasted_iota(jnp.int32, (1, order_count), 1)
    place = jnp.where(column < order_ref[0, 0, 0], place, -1)
    index = lax.broadcasted_iota(jnp.int32, (owned, 1), 0)
    for slot in range(len(remote) + 1):
        pick[slot] = jnp.where(place == index + slot * owned, 1.0, 0.0).astype(BF16)
    weight = deluxe_ref[0]

    def transpose_pick():
        spread = jnp.broadcast_to(place.astype(F32), (128, order_count)).T.astype(jnp.int32)
        lane = lax.broadcasted_iota(jnp.int32, (1, 128), 1)
        for at_column in range(0, place_back.shape[1], 128):
            found = jnp.where(spread == lane + at_column, 1.0, 0.0)
            place_back[:, at_column : at_column + 128] = found.astype(BF16)


    def prepare(matrix, high, low):
        step = 128

        def some(i, carry):
            part = pl.ds(pl.multiple_of(i * step, step), step)
            high[part, :], low[part, :] = split(matrix[part, :])
            return carry

        lax.fori_loop(0, order_count // step, some, 0)

    def gather(stage, own):
        def add(slot, block):
            high, low = split(block)
            both = jnp.concatenate([high, low], axis=0)
            part = jnp.dot(both, pick[slot], preferred_element_type=F32)
            if slot == 0:
                local[...] = part
            else:
                local[...] += part

        add(0, own)
        for slot in reversed(slots):
            present(slot, lambda slot=slot: copy_from(stage, slot).wait_recv())
            add(slot, landed[stage, slot - 1])

    def apply(turn, own, high, low, scaled):
        gather(2 * turn, own)
        value = local[:rows] + local[rows:]
        if scaled:
            value = value * weight
        value_high, value_low = split(value)
        stacked[:rows] = value_high
        stacked[rows:] = value_low
        for part in range(0, order_count, wide):
            columns = slice(part, part + wide)
            main = jnp.dot(stacked[...], high[:, columns], preferred_element_type=F32)
            rest = jnp.dot(stacked[:rows], low[:, columns], preferred_element_type=F32)
            image = main[:rows] + main[rows:] + rest
            if scaled:
                image = image * weight[:, columns]
            image_high, image_low = split(image)
            images[:rows, columns] = image_high
            images[rows:, columns] = image_low

        def scatter(slot):
            back = place_back[:, slot * owned : (slot + 1) * owned]
            both = jnp.dot(images[...], back, preferred_element_type=F32)
            return both[:rows] + both[rows:]

        for slot in slots:
            contrib[turn, slot - 1] = scatter(slot)
            present(
                slot,
                lambda slot=slot: copy_to(2 * turn + 1, slot, contrib.at[turn, slot - 1]).start(),
            )
        return scatter(0)

    def returned(turn, total):
        for slot in reversed(slots):
            present(slot, lambda slot=slot: copy_from(2 * turn + 1, slot).wait_recv())
            total = total + landed[2 * turn + 1, slot - 1]
        return total

    transpose_pick()
    load_inverse.wait()
    load_schur.start()
    prepare(inverse, inverse_high, inverse_low)
    own = apply(0, seeds[...], inverse_high, inverse_low, True)
    load_schur.wait()
    prepare(schur, schur_high, schur_low)
    first[...] = returned(0, own)
    send_all(2, first)

    own = apply(1, first[...], schur_high, schur_low, False)
    residual_ref[...] = seeds[...] - returned(1, own)
    send_all(4, residual_ref)

    own = apply(2, residual_ref[...], inverse_high, inverse_low, True)
    adjoint_ref[...] = first[...] + returned(2, own)

    for stage, source in enumerate((seeds, None, first, None, residual_ref, None)):
        for slot in slots:
            block = contrib.at[stage // 2, slot - 1] if source is None else source
            present(
                slot,
                lambda stage=stage, slot=slot, block=block: copy_to(stage, slot, block).wait_send(),
            )


def hand_over(adjoint, residual, adjoint_out, residual_out, sems):
    one = pltpu.make_async_copy(adjoint, adjoint_out, sems.at[0])
    two = pltpu.make_async_copy(residual, residual_out, sems.at[1])
    one.start()
    two.start()
    one.wait()
    two.wait()


def solution(mesh):
    sizes = tuple(mesh.shape[name] for name in AXES)
    remote, kept = slot_plan(sizes)

    def body(seeds, schur, inverse, deluxe, orders, links):
        rows, owned = seeds.shape[3:]
        order_count = schur.shape[3]
        count = len(remote)
        vmem = pl.BlockSpec(memory_space=pltpu.VMEM)
        hbm = pl.BlockSpec(memory_space=pl.ANY)
        result = jax.ShapeDtypeStruct((rows, owned), F32)
        square = (order_count, order_count)
        adjoint, residual = pl.pallas_call(
            functools.partial(kernel, sizes, remote, kept),
            out_shape=(result, result),
            in_specs=[vmem, hbm, hbm, vmem, pl.BlockSpec(memory_space=pltpu.SMEM), vmem],
            out_specs=(vmem, vmem),
            scratch_shapes=[
                pltpu.VMEM(square, F32),
                pltpu.VMEM(square, F32),
                pltpu.VMEM(square, BF16),
                pltpu.VMEM(square, BF16),
                pltpu.VMEM(square, BF16),
                pltpu.VMEM(square, BF16),
                pltpu.VMEM((count + 1, owned, order_count), BF16),
                pltpu.VMEM((order_count, (count + 1) * owned), BF16),
                pltpu.VMEM((6, count, rows, owned), F32),
                pltpu.VMEM((3, count, rows, owned), F32),
                pltpu.VMEM((rows, owned), F32),
                pltpu.VMEM((2 * rows, order_count), BF16),
                pltpu.VMEM((2 * rows, order_count), BF16),
                pltpu.VMEM((2 * rows, order_count), F32),
                pltpu.SemaphoreType.DMA((2,)),
                pltpu.SemaphoreType.DMA((6, count)),
                pltpu.SemaphoreType.DMA((6, count)),
            ],
            compiler_params=pltpu.CompilerParams(
                collective_id=0, has_side_effects=True, vmem_limit_bytes=60 * 1024 * 1024
            ),
        )(
            seeds[0, 0, 0],
            schur[0, 0, 0],
            inverse[0, 0, 0],
            deluxe[0],
            orders,
            links[0],
        )
        adjoint, residual = pl.pallas_call(
            hand_over,
            out_shape=(result, result),
            in_specs=[hbm, hbm],
            out_specs=(hbm, hbm),
            scratch_shapes=[pltpu.SemaphoreType.DMA((2,))],
        )(adjoint, residual)
        return adjoint[None, None, None], residual[None, None, None]

    in_specs = (
        P("gx", "gy", "gz", None, None),
        P("gx", "gy", "gz", None, None),
        P("gx", "gy", "gz", None, None),
        P("gx", "gy", "gz", None),
        P("gx", "gy", "gz"),
        P("gx", "gy", "gz", None),
    )
    out_specs = (P("gx", "gy", "gz", None, None), P("gx", "gy", "gz", None, None))
    return jax.shard_map(body, mesh=mesh, in_specs=in_specs, out_specs=out_specs, check_vma=False)
```

```python
import functools

import jax
import jax.numpy as jnp
from jax import lax
from jax.experimental import pallas as pl
from jax.experimental.pallas import tpu as pltpu
from jax.sharding import PartitionSpec as P

MESH = pl.DeviceIdType.MESH
F32 = jnp.float32
BF16 = jnp.bfloat16
AXES = ("gx", "gy", "gz")


def slot_plan(sizes):
    remote, kept = [], [0]
    for at, size in enumerate(sizes):
        here = 1 + len(remote)
        if size == 2:
            remote.append((at, 0, here))
            kept += [here, here]
        else:
            remote += [(at, -1, here + 1), (at, 1, here)]
            kept += [here, here + 1]
    return remote, kept


def split(value):
    high = value.astype(BF16)
    return high, (value - high.astype(F32)).astype(BF16)


def kernel(
    sizes,
    remote,
    kept,
    seeds,
    schur_hbm,
    inverse_hbm,
    deluxe_ref,
    order_ref,
    links_ref,
    adjoint_ref,
    residual_ref,
    schur,
    inverse,
    schur_high,
    schur_low,
    inverse_high,
    inverse_low,
    pick,
    place_back,
    landed,
    contrib,
    first,
    stacked,
    images,
    local,
    load_sem,
    send_sem,
    recv_sem,
):
    rows, owned = seeds.shape
    order_count = schur.shape[0]
    wide = 384 if order_count % 384 == 0 else 128
    at = [lax.axis_index(name) for name in AXES]

    def neighbour(slot):
        axis, step, _ = remote[slot - 1]
        there = list(at)
        there[axis] = 1 - at[axis] if step == 0 else at[axis] + step
        return tuple(there)

    def present(slot, run, otherwise=None):
        axis, step, _ = remote[slot - 1]
        if step == 0:
            run()
            return
        there = at[axis] > 0 if step < 0 else at[axis] < sizes[axis] - 1
        pl.when(there)(run)
        if otherwise is not None:
            pl.when(jnp.logical_not(there))(otherwise)

    slots = range(1, len(remote) + 1)

    def copy_to(stage, slot, source):
        there = remote[slot - 1][2]
        return pltpu.make_async_remote_copy(
            src_ref=source,
            dst_ref=landed.at[stage, there - 1],
            send_sem=send_sem.at[stage, slot - 1],
            recv_sem=recv_sem.at[stage, there - 1],
            device_id=neighbour(slot),
            device_id_type=MESH,
        )

    def copy_from(stage, slot):
        return pltpu.make_async_remote_copy(
            src_ref=landed.at[stage, slot - 1],
            dst_ref=landed.at[stage, slot - 1],
            send_sem=send_sem.at[stage, slot - 1],
            recv_sem=recv_sem.at[stage, slot - 1],
            device_id=neighbour(slot),
            device_id_type=MESH,
        )

    load_inverse = pltpu.make_async_copy(inverse_hbm, inverse, load_sem.at[0])
    load_schur = pltpu.make_async_copy(schur_hbm, schur, load_sem.at[1])
    load_inverse.start()

    barrier = pltpu.get_barrier_semaphore()
    for slot in slots:
        present(
            slot,
            lambda slot=slot: pl.semaphore_signal(
                barrier, inc=1, device_id=neighbour(slot), device_id_type=MESH
            ),
        )
    peers = 0
    for axis, step, _ in remote:
        if step == 0:
            peers += 1
        else:
            there = at[axis] > 0 if step < 0 else at[axis] < sizes[axis] - 1
            peers += jnp.where(there, 1, 0)
    pl.semaphore_wait(barrier, peers)

    def send_all(stage, source):
        for slot in slots:
            present(slot, lambda slot=slot: copy_to(stage, slot, source).start())

    send_all(0, seeds)

    for slot in slots:

        def clear(slot=slot):
            for stage in range(6):
                landed[stage, slot - 1] = jnp.zeros((rows, owned), F32)

        present(slot, lambda: None, clear)

    links = links_ref[0]
    place = links
    for slot, here in enumerate(kept):
        if here != slot:
            inside = jnp.logical_and(links >= slot * owned, links < (slot + 1) * owned)
            place = jnp.where(inside, links + (here - slot) * owned, place)
    column = lax.broadcasted_iota(jnp.int32, (1, order_count), 1)
    place = jnp.where(column < order_ref[0, 0, 0], place, -1)
    index = lax.broadcasted_iota(jnp.int32, (owned, 1), 0)
    for slot in range(len(remote) + 1):
        pick[slot] = jnp.where(place == index + slot * owned, 1.0, 0.0).astype(BF16)
    weight = deluxe_ref[0]

    def transpose_pick():
        spread = jnp.broadcast_to(place.astype(F32), (128, order_count)).T.astype(jnp.int32)
        lane = lax.broadcasted_iota(jnp.int32, (1, 128), 1)
        for at_column in range(0, place_back.shape[1], 128):
            found = jnp.where(spread == lane + at_column, 1.0, 0.0)
            place_back[:, at_column : at_column + 128] = found.astype(BF16)


    def prepare(matrix, high, low):
        step = 128

        def some(i, carry):
            part = pl.ds(pl.multiple_of(i * step, step), step)
            high[part, :], low[part, :] = split(matrix[part, :])
            return carry

        lax.fori_loop(0, order_count // step, some, 0)

    def gather(stage, own):
        def add(slot, block):
            high, low = split(block)
            both = jnp.concatenate([high, low], axis=0)
            part = jnp.dot(both, pick[slot], preferred_element_type=F32)
            if slot == 0:
                local[...] = part
            else:
                local[...] += part

        add(0, own)
        for slot in reversed(slots):
            present(slot, lambda slot=slot: copy_from(stage, slot).wait_recv())
            add(slot, landed[stage, slot - 1])

    def apply(turn, own, high, low, scaled):
        gather(2 * turn, own)
        value = local[:rows] + local[rows:]
        if scaled:
            value = value * weight
        value_high, value_low = split(value)
        stacked[:rows] = value_high
        stacked[rows:] = value_low
        for part in range(0, order_count, wide):
            columns = slice(part, part + wide)
            main = jnp.dot(stacked[...], high[:, columns], preferred_element_type=F32)
            rest = jnp.dot(stacked[:rows], low[:, columns], preferred_element_type=F32)
            image = main[:rows] + main[rows:] + rest
            if scaled:
                image = image * weight[:, columns]
            image_high, image_low = split(image)
            images[:rows, columns] = image_high
            images[rows:, columns] = image_low

        def scatter(slot):
            back = place_back[:, slot * owned : (slot + 1) * owned]
            both = jnp.dot(images[...], back, preferred_element_type=F32)
            return both[:rows] + both[rows:]

        for slot in slots:
            contrib[turn, slot - 1] = scatter(slot)
            present(
                slot,
                lambda slot=slot: copy_to(2 * turn + 1, slot, contrib.at[turn, slot - 1]).start(),
            )
        return scatter(0)

    def returned(turn, total):
        for slot in reversed(slots):
            present(slot, lambda slot=slot: copy_from(2 * turn + 1, slot).wait_recv())
            total = total + landed[2 * turn + 1, slot - 1]
        return total

    transpose_pick()
    load_inverse.wait()
    load_schur.start()
    prepare(inverse, inverse_high, inverse_low)
    own = apply(0, seeds[...], inverse_high, inverse_low, True)
    load_schur.wait()
    prepare(schur, schur_high, schur_low)
    first[...] = returned(0, own)
    send_all(2, first)

    own = apply(1, first[...], schur_high, schur_low, False)
    residual_ref[...] = seeds[...] - returned(1, own)
    send_all(4, residual_ref)

    own = apply(2, residual_ref[...], inverse_high, inverse_low, True)
    adjoint_ref[...] = first[...] + returned(2, own)

    for stage, source in enumerate((seeds, None, first, None, residual_ref, None)):
        for slot in slots:
            block = contrib.at[stage // 2, slot - 1] if source is None else source
            present(
                slot,
                lambda stage=stage, slot=slot, block=block: copy_to(stage, slot, block).wait_send(),
            )


def hand_over(adjoint, residual, adjoint_out, residual_out):
    adjoint_out[...] = adjoint[...]
    residual_out[...] = residual[...]


def solution(mesh):
    sizes = tuple(mesh.shape[name] for name in AXES)
    remote, kept = slot_plan(sizes)

    def body(seeds, schur, inverse, deluxe, orders, links):
        rows, owned = seeds.shape[3:]
        order_count = schur.shape[3]
        count = len(remote)
        vmem = pl.BlockSpec(memory_space=pltpu.VMEM)
        hbm = pl.BlockSpec(memory_space=pl.ANY)
        result = jax.ShapeDtypeStruct((rows, owned), F32)
        square = (order_count, order_count)
        adjoint, residual = pl.pallas_call(
            functools.partial(kernel, sizes, remote, kept),
            out_shape=(result, result),
            in_specs=[vmem, hbm, hbm, vmem, pl.BlockSpec(memory_space=pltpu.SMEM), vmem],
            out_specs=(vmem, vmem),
            scratch_shapes=[
                pltpu.VMEM(square, F32),
                pltpu.VMEM(square, F32),
                pltpu.VMEM(square, BF16),
                pltpu.VMEM(square, BF16),
                pltpu.VMEM(square, BF16),
                pltpu.VMEM(square, BF16),
                pltpu.VMEM((count + 1, owned, order_count), BF16),
                pltpu.VMEM((order_count, (count + 1) * owned), BF16),
                pltpu.VMEM((6, count, rows, owned), F32),
                pltpu.VMEM((3, count, rows, owned), F32),
                pltpu.VMEM((rows, owned), F32),
                pltpu.VMEM((2 * rows, order_count), BF16),
                pltpu.VMEM((2 * rows, order_count), BF16),
                pltpu.VMEM((2 * rows, order_count), F32),
                pltpu.SemaphoreType.DMA((2,)),
                pltpu.SemaphoreType.DMA((6, count)),
                pltpu.SemaphoreType.DMA((6, count)),
            ],
            compiler_params=pltpu.CompilerParams(
                collective_id=0, has_side_effects=True, vmem_limit_bytes=60 * 1024 * 1024
            ),
        )(
            seeds[0, 0, 0],
            schur[0, 0, 0],
            inverse[0, 0, 0],
            deluxe[0],
            orders,
            links[0],
        )
        adjoint, residual = pl.pallas_call(
            hand_over,
            out_shape=(result, result),
            in_specs=[vmem, vmem],
            out_specs=(vmem, vmem),
        )(adjoint, residual)
        return adjoint[None, None, None], residual[None, None, None]

    in_specs = (
        P("gx", "gy", "gz", None, None),
        P("gx", "gy", "gz", None, None),
        P("gx", "gy", "gz", None, None),
        P("gx", "gy", "gz", None),
        P("gx", "gy", "gz"),
        P("gx", "gy", "gz", None),
    )
    out_specs = (P("gx", "gy", "gz", None, None), P("gx", "gy", "gz", None, None))
    return jax.shard_map(body, mesh=mesh, in_specs=in_specs, out_specs=out_specs, check_vma=False)
```
